32 devices in a mesh: row: 4 (over y, core), col: 8 (over z, x).
Axes of the slice: x: 2, y: 2, z: 4, core: 2. Of those that a mesh axis runs over, the one named last changes fastest.
Arguments:
- inputs: bfloat16 [192, 8192], P('col', 'row'), may hold values from -6 to 6
- w_gate: bfloat16 [8192, 14336], P('row', 'col'), may hold values from -0.0625 to 0.0625
- w_up: bfloat16 [8192, 14336], P('row', 'col'), may hold values from -0.0625 to 0.0625
- w_down: bfloat16 [14336, 8192], P('col', 'row'), may hold values from -0.046875 to 0.046875
- cotangent: bfloat16 [192, 8192], P('col', 'row'), may hold values from -6 to 6
Outputs:
- grad_inputs: bfloat16 [192, 8192], P('col', 'row')
- grad_gate: bfloat16 [8192, 14336], P('row', 'col')
- grad_up: bfloat16 [8192, 14336], P('row', 'col')
- grad_down: bfloat16 [14336, 8192], P('col', 'row')
The draws below stay inside these ranges and needn't reach their ends.
All inputs are finite; a program needn't handle non-finite values.
Results may differ from the reference program's by a relative error of at most 0.0049.
Values may be sent and summed in bfloat16 or wider, within the bound.
A program may use at most 128 MiB of HBM per device.

```python
import jax
import jax.numpy as jnp

D = 8192
FF_WIN = 14336
TOKENS = 192


def shard_levels(key, dims, cuts, smallest, high):
    gain, own = 1.0, jax.random.fold_in(key, 6)
    for axis_at, parts in cuts:
        draws = jnp.exp(jax.random.uniform(jax.random.fold_in(own, axis_at), (parts,), jnp.float32, smallest / len(cuts), high / len(cuts)))
        gain = gain * jnp.repeat(draws, dims[axis_at] // parts).reshape([-1 if axis == axis_at else 1 for axis in range(len(dims))])
    return gain


def bell_draw(key, extent, scale, most, cuts=(), held_as=jnp.bfloat16):
    factor_of = shard_levels(key, extent, cuts, -0.22, 0.18) if cuts else 1.0
    values = jax.random.normal(key, extent, jnp.float32) * scale * factor_of
    return jnp.minimum(jnp.maximum(values, -most), most).astype(held_as)


def setup_inputs(seed: int = 0) -> dict:
    arg_keys = jax.random.split(jax.random.key(seed), 6)
    return {
        "inputs": bell_draw(arg_keys[0], (TOKENS, D), 1.0, 6.0, ((0, 8), (1, 4))),
        "w_gate": bell_draw(arg_keys[1], (D, FF_WIN), D ** -0.5, 0.0625, ((0, 4), (1, 8))),
        "w_up": bell_draw(arg_keys[2], (D, FF_WIN), D ** -0.5, 0.0625, ((0, 4), (1, 8))),
        "w_down": bell_draw(arg_keys[3], (FF_WIN, D), FF_WIN ** -0.5, 0.046875, ((0, 8), (1, 4))),
        "cotangent": bell_draw(arg_keys[4], (TOKENS, D), 1.0, 6.0, ((0, 8), (1, 4))),
    }


def reference(inputs, w_gate, w_up, w_down, cotangent):
    gate_sum = jnp.dot(inputs, w_gate, preferred_element_type=jnp.float32)
    up_sum = jnp.dot(inputs, w_up, preferred_element_type=jnp.float32)
    grad_hidden = jnp.dot(cotangent, w_down.T, preferred_element_type=jnp.float32)
    sigmoid_gate = jax.nn.sigmoid(gate_sum)
    activated = gate_sum * sigmoid_gate
    hidden = (activated * up_sum).astype(jnp.bfloat16)
    grad_gate_act = (grad_hidden * up_sum * sigmoid_gate * (1.0 + gate_sum * (1.0 - sigmoid_gate))).astype(jnp.bfloat16)
    grad_up_act = (grad_hidden * activated).astype(jnp.bfloat16)
    grad_inputs = (jnp.dot(grad_gate_act, w_gate.T, preferred_element_type=jnp.float32)
                   + jnp.dot(grad_up_act, w_up.T, preferred_element_type=jnp.float32)).astype(jnp.bfloat16)
    grad_gate = jnp.dot(inputs.T, grad_gate_act, preferred_element_type=jnp.float32).astype(jnp.bfloat16)
    grad_up = jnp.dot(inputs.T, grad_up_act, preferred_element_type=jnp.float32).astype(jnp.bfloat16)
    grad_down = jnp.dot(hidden.T, cotangent, preferred_element_type=jnp.float32).astype(jnp.bfloat16)
    return grad_inputs, grad_gate, grad_up, grad_down
```

```python
import jax
import jax.numpy as jnp
from jax import lax
from jax.experimental import pallas as pl
from jax.experimental.pallas import tpu as pltpu
from jax.sharding import PartitionSpec as P

MESH = pl.DeviceIdType.MESH
BF16, F32 = jnp.bfloat16, jnp.float32
TILE = 256


def contract_rows(left, right):
    return lax.dot_general(
        left, right, (((0,), (0,)), ((), ())), preferred_element_type=jnp.float32
    )


def contract_cols(left, right):
    return lax.dot_general(
        left, right, (((1,), (1,)), ((), ())), preferred_element_type=jnp.float32
    )


def activations(gate_sum, up_sum, grad_hidden):
    sigmoid_gate = jax.nn.sigmoid(gate_sum)
    activated = gate_sum * sigmoid_gate
    hidden = (activated * up_sum).astype(BF16)
    grad_gate_act = (
        grad_hidden * up_sum * sigmoid_gate * (1.0 + gate_sum * (1.0 - sigmoid_gate))
    ).astype(BF16)
    grad_up_act = (grad_hidden * activated).astype(BF16)
    return grad_gate_act, grad_up_act, hidden


def on_device(inputs, w_gate, w_up, w_down, cotangent):
    rows_in = lax.all_gather(inputs, "col", axis=0, tiled=True)
    rows_co = lax.all_gather(cotangent, "col", axis=0, tiled=True)
    columns = w_gate.shape[1]
    gate_part = jnp.dot(rows_in, w_gate, preferred_element_type=jnp.float32)
    up_part = jnp.dot(rows_in, w_up, preferred_element_type=jnp.float32)
    back_part = contract_cols(rows_co, w_down)
    summed = lax.psum_scatter(
        jnp.concatenate([gate_part, up_part, back_part], axis=1),
        "row",
        scatter_dimension=0,
        tiled=True,
    )
    acts = activations(
        summed[:, :columns], summed[:, columns : 2 * columns], summed[:, 2 * columns :]
    )
    piece_gate, piece_up, piece_hidden = [
        lax.all_gather(act, "row", axis=0, tiled=True) for act in acts
    ]
    acc_gate = contract_rows(rows_in, piece_gate)
    acc_up = contract_rows(rows_in, piece_up)
    acc_down = contract_rows(piece_hidden, rows_co)
    acc_inputs = contract_cols(piece_gate, w_gate) + contract_cols(piece_up, w_up)
    grad_inputs = lax.psum_scatter(acc_inputs, "col", scatter_dimension=0, tiled=True)
    return (
        grad_inputs.astype(BF16),
        acc_gate.astype(BF16),
        acc_up.astype(BF16),
        acc_down.astype(BF16),
    )


def block_kernel(
    in_ref, cot_ref, wg_hbm, wu_hbm, wd_hbm,
    x_out, c_out, act_out, gi_ref,
    got, wg, wu, wd, xs, cs, part, sib_got, y_send, y_got, act,
    keep, rx_send, rx_got, rz_send, rz_got,
    load_sem, out_sem, z_ss, z_rs, x_ss, x_rs, p_ss, p_rs, y_ss, y_rs, a_ss, a_rs,
    gx_ss, gx_rs, gz_ss, gz_rs,
):
    shard, width = in_ref.shape
    half = 4 * shard
    mine = half // 2
    tiles = wg.shape[1] // TILE
    r, c = lax.axis_index("row"), lax.axis_index("col")
    k, x, z = lax.rem(r, 2), lax.rem(c, 2), lax.div(c, 2)
    sibling = (r + 1 - 2 * k, c)
    over_y = (lax.rem(r + 2, 4), c)
    over_x = (r, c + 1 - 2 * x)
    flipped = [z, z + 1 - 2 * lax.rem(z, 2), lax.rem(z + 2, 4), 3 - z]
    over_z = [(r, 2 * f + x) for f in flipped]
    own_rows = pl.multiple_of(k * mine, 16)
    sib_rows = pl.multiple_of((1 - k) * mine, 16)

    loads = [
        pltpu.make_async_copy(src, dst, load_sem.at[i])
        for i, (src, dst) in enumerate(
            [(in_ref, got.at[0, 0]), (cot_ref, got.at[0, 1]), (wg_hbm, wg), (wu_hbm, wu), (wd_hbm, wd)]
        )
    ]
    for load in loads:
        load.start()

    barrier = pltpu.get_barrier_semaphore()
    partners = [sibling, over_y, over_x] + over_z[1:]
    for partner in partners:
        pl.semaphore_signal(barrier, inc=1, device_id=partner, device_id_type=MESH)
    pl.semaphore_wait(barrier, len(partners))

    def remote(src, dst, ss, rs, device):
        return pltpu.make_async_remote_copy(
            src_ref=src, dst_ref=dst, send_sem=ss, recv_sem=rs, device_id=device, device_id_type=MESH
        )

    to_z = [None] + [
        remote(got.at[0], got.at[2 * d], z_ss.at[d], z_rs.at[d], over_z[d]) for d in (1, 2, 3)
    ]
    to_x = [
        remote(got.at[2 * d], got.at[2 * d + 1], x_ss.at[d], x_rs.at[d], over_x) for d in range(4)
    ]

    loads[0].wait()
    loads[1].wait()
    to_z[1].start()
    to_x[0].start()
    to_z[1].wait_recv()
    to_x[1].start()
    to_z[1].wait_send()
    to_z[3].start()
    to_z[2].start()

    def settle(h):
        at = pl.ds(h * half, half)
        for i, whole in enumerate((xs, cs)):
            whole[at, :] = jnp.concatenate(
                [got[4 * h + s, i].astype(F32) for s in range(4)], axis=0
            ).astype(BF16)

    def to_sibling(h, j):
        return remote(
            part.at[h, j, :, pl.ds(sib_rows, mine), :], sib_got.at[h, j],
            p_ss.at[h, j], p_rs.at[h, j], sibling,
        )

    def to_y(h, j):
        return remote(y_send.at[h, j], y_got.at[h, j], y_ss.at[h, j], y_rs.at[h, j], over_y)

    def act_to_sibling(h, j):
        at = act.at[:, pl.ds(pl.multiple_of(h * half + own_rows, 16), mine), pl.ds(pl.multiple_of(j * TILE, TILE), TILE)]
        return remote(at, at, a_ss.at[h, j], a_rs.at[h, j], sibling)

    def forward(h):
        at = pl.ds(h * half, half)

        @pl.loop(0, tiles)
        def _(j):
            cols = pl.ds(pl.multiple_of(j * TILE, TILE), TILE)
            part[h, j, 0] = jnp.dot(xs[at, :], wg[:, cols], preferred_element_type=F32)
            part[h, j, 1] = jnp.dot(xs[at, :], wu[:, cols], preferred_element_type=F32)
            part[h, j, 2] = contract_cols(cs[at, :], wd[cols, :])
            to_sibling(h, j).start()

    def reduce_cores(h):
        @pl.loop(0, tiles)
        def _(j):
            to_sibling(h, j).wait_recv()
            total = part[h, j, :, pl.ds(own_rows, mine), :] + sib_got[h, j]
            part[h, j, :, pl.ds(own_rows, mine), :] = total
            y_send[h, j] = total.astype(BF16)
            to_y(h, j).start()

    def activate(h):
        @pl.loop(0, tiles)
        def _(j):
            to_y(h, j).wait_recv()
            total = part[h, j, :, pl.ds(own_rows, mine), :] + y_got[h, j].astype(F32)
            rows = pl.ds(pl.multiple_of(h * half + own_rows, 16), mine)
            cols = pl.ds(pl.multiple_of(j * TILE, TILE), TILE)
            for m, value in enumerate(activations(total[0], total[1], total[2])):
                act[m, rows, cols] = value
            act_to_sibling(h, j).start()

        @pl.loop(0, tiles)
        def _(j):
            act_to_sibling(h, j).wait_recv()

    def grad_to_x(d):
        return remote(rx_send.at[d], rx_got.at[d], gx_ss.at[d], gx_rs.at[d], over_x)

    def grad_to_z(d):
        return remote(rz_send.at[d], rz_got.at[d], gz_ss.at[d], gz_rs.at[d], over_z[d])

    def backward(h):
        at = pl.ds(h * half, half)

        @pl.loop(0, width // TILE)
        def _(j):
            cols = pl.ds(pl.multiple_of(j * TILE, TILE), TILE)
            grad = contract_cols(act[0, at, :], wg[cols, :]) + contract_cols(act[1, at, :], wu[cols, :])
            for e in range(2):
                d = 2 * h + e
                keep[d, :, cols] = grad[2 * e * shard : (2 * e + 1) * shard]
                rx_send[d, :, cols] = grad[(2 * e + 1) * shard : (2 * e + 2) * shard].astype(BF16)

        for e in range(2):
            grad_to_x(2 * h + e).start()

    def reduce_x(h):
        for e in range(2):
            d = 2 * h + e
            grad_to_x(d).wait_recv()
            total = keep[d] + rx_got[d].astype(F32)
            if d == 0:
                keep[d] = total
            else:
                rz_send[d] = total.astype(BF16)
                grad_to_z(d).start()

    to_x[0].wait_recv()
    to_x[1].wait_recv()
    settle(0)
    for load in loads[2:]:
        load.wait()
    forward(0)
    reduce_cores(0)
    to_z[3].wait_recv()
    to_x[3].start()
    to_z[2].wait_recv()
    to_x[2].start()
    to_x[3].wait_recv()
    to_x[2].wait_recv()
    settle(1)
    outs = [
        pltpu.make_async_copy(src, dst, out_sem.at[i])
        for i, (src, dst) in enumerate([(xs, x_out), (cs, c_out), (act, act_out)])
    ]
    outs[0].start()
    outs[1].start()
    forward(1)
    reduce_cores(1)
    activate(0)
    backward(0)
    reduce_x(0)
    activate(1)
    outs[2].start()
    backward(1)
    reduce_x(1)
    total = keep[0]
    for d in (1, 3, 2):
        grad_to_z(d).wait_recv()
        total += rz_got[d].astype(F32)
    gi_ref[...] = total.astype(BF16)

    for d in (1, 2, 3):
        grad_to_z(d).wait_send()
        if d > 1:
            to_z[d].wait_send()
    for d in range(4):
        to_x[d].wait_send()
        grad_to_x(d).wait_send()
    for h in range(2):
        @pl.loop(0, tiles)
        def _(j):
            to_sibling(h, j).wait_send()
            to_y(h, j).wait_send()
            act_to_sibling(h, j).wait_send()
    for out in outs:
        out.wait()


def fused(inputs, w_gate, w_up, w_down, cotangent):
    shard, width = inputs.shape
    columns = w_gate.shape[1]
    tokens = 8 * shard
    half, mine, tiles = tokens // 2, tokens // 4, columns // TILE
    dma = pltpu.SemaphoreType.DMA
    hbm = pl.BlockSpec(memory_space=pl.ANY)
    xs, cs, act, grad_inputs = pl.pallas_call(
        block_kernel,
        out_shape=(
            jax.ShapeDtypeStruct((tokens, width), BF16),
            jax.ShapeDtypeStruct((tokens, width), BF16),
            jax.ShapeDtypeStruct((3, tokens, columns), BF16),
            jax.ShapeDtypeStruct((shard, width), BF16),
        ),
        in_specs=[hbm] * 5,
        out_specs=(hbm, hbm, hbm, pl.BlockSpec(memory_space=pltpu.VMEM)),
        scratch_shapes=[
            pltpu.VMEM((8, 2, shard, width), BF16),
            pltpu.VMEM(w_gate.shape, BF16),
            pltpu.VMEM(w_up.shape, BF16),
            pltpu.VMEM(w_down.shape, BF16),
            pltpu.VMEM((tokens, width), BF16),
            pltpu.VMEM((tokens, width), BF16),
            pltpu.VMEM((2, tiles, 3, half, TILE), F32),
            pltpu.VMEM((2, tiles, 3, mine, TILE), F32),
            pltpu.VMEM((2, tiles, 3, mine, TILE), BF16),
            pltpu.VMEM((2, tiles, 3, mine, TILE), BF16),
            pltpu.VMEM((3, tokens, columns), BF16),
            pltpu.VMEM((4, shard, width), F32),
            pltpu.VMEM((4, shard, width), BF16),
            pltpu.VMEM((4, shard, width), BF16),
            pltpu.VMEM((4, shard, width), BF16),
            pltpu.VMEM((4, shard, width), BF16),
            dma((5,)), dma((3,)), dma((4,)), dma((4,)), dma((4,)), dma((4,)),
            dma((2, tiles)), dma((2, tiles)), dma((2, tiles)), dma((2, tiles)),
            dma((2, tiles)), dma((2, tiles)),
            dma((4,)), dma((4,)), dma((4,)), dma((4,)),
        ],
        compiler_params=pltpu.CompilerParams(
            collective_id=0, has_side_effects=True, vmem_limit_bytes=56 * 2**20
        ),
        name="swiglu_block",
    )(inputs, cotangent, w_gate, w_up, w_down)
    return (
        grad_inputs,
        contract_rows(xs, act[0]).astype(BF16),
        contract_rows(xs, act[1]).astype(BF16),
        contract_rows(act[2], cs).astype(BF16),
    )


def solution(mesh):
    placed = (P("col", "row"), P("row", "col"), P("row", "col"), P("col", "row"), P("col", "row"))
    small = mesh.shape["row"] == 4 and mesh.shape["col"] == 8
    return jax.shard_map(
        fused if small else on_device,
        mesh=mesh,
        in_specs=placed,
        out_specs=(P("col", "row"), P("row", "col"), P("row", "col"), P("col", "row")),
        check_vma=False,
    )
```

```python
import jax
import jax.numpy as jnp
from jax import lax
from jax.experimental import pallas as pl
from jax.experimental.pallas import tpu as pltpu
from jax.sharding import PartitionSpec as P

MESH = pl.DeviceIdType.MESH
BF16, F32 = jnp.bfloat16, jnp.float32
TILE = 256


def contract_rows(left, right):
    return lax.dot_general(
        left, right, (((0,), (0,)), ((), ())), preferred_element_type=jnp.float32
    )


def contract_cols(left, right):
    return lax.dot_general(
        left, right, (((1,), (1,)), ((), ())), preferred_element_type=jnp.float32
    )


def activations(gate_sum, up_sum, grad_hidden):
    sigmoid_gate = jax.nn.sigmoid(gate_sum)
    activated = gate_sum * sigmoid_gate
    hidden = (activated * up_sum).astype(BF16)
    grad_gate_act = (
        grad_hidden * up_sum * sigmoid_gate * (1.0 + gate_sum * (1.0 - sigmoid_gate))
    ).astype(BF16)
    grad_up_act = (grad_hidden * activated).astype(BF16)
    return grad_gate_act, grad_up_act, hidden


def on_device(inputs, w_gate, w_up, w_down, cotangent):
    rows_in = lax.all_gather(inputs, "col", axis=0, tiled=True)
    rows_co = lax.all_gather(cotangent, "col", axis=0, tiled=True)
    columns = w_gate.shape[1]
    gate_part = jnp.dot(rows_in, w_gate, preferred_element_type=jnp.float32)
    up_part = jnp.dot(rows_in, w_up, preferred_element_type=jnp.float32)
    back_part = contract_cols(rows_co, w_down)
    summed = lax.psum_scatter(
        jnp.concatenate([gate_part, up_part, back_part], axis=1),
        "row",
        scatter_dimension=0,
        tiled=True,
    )
    acts = activations(
        summed[:, :columns], summed[:, columns : 2 * columns], summed[:, 2 * columns :]
    )
    piece_gate, piece_up, piece_hidden = [
        lax.all_gather(act, "row", axis=0, tiled=True) for act in acts
    ]
    acc_gate = contract_rows(rows_in, piece_gate)
    acc_up = contract_rows(rows_in, piece_up)
    acc_down = contract_rows(piece_hidden, rows_co)
    acc_inputs = contract_cols(piece_gate, w_gate) + contract_cols(piece_up, w_up)
    grad_inputs = lax.psum_scatter(acc_inputs, "col", scatter_dimension=0, tiled=True)
    return (
        grad_inputs.astype(BF16),
        acc_gate.astype(BF16),
        acc_up.astype(BF16),
        acc_down.astype(BF16),
    )


def block_kernel(
    in_ref, cot_ref, wg_hbm, wu_hbm, wd_hbm,
    x_out, c_out, act_out, gi_ref,
    got, wg, wu, wd, xs, cs, part, sib_got, y_send, y_got, act,
    grads, keep, rx_send, rx_got, rz_send, rz_got,
    load_sem, out_sem, z_ss, z_rs, x_ss, x_rs, p_ss, p_rs, y_ss, y_rs, a_ss, a_rs,
    gx_ss, gx_rs, gz_ss, gz_rs,
):
    shard, width = in_ref.shape
    half = 4 * shard
    mine = half // 2
    tiles = wg.shape[1] // TILE
    r, c = lax.axis_index("row"), lax.axis_index("col")
    k, x, z = lax.rem(r, 2), lax.rem(c, 2), lax.div(c, 2)
    sibling = (r + 1 - 2 * k, c)
    over_y = (lax.rem(r + 2, 4), c)
    over_x = (r, c + 1 - 2 * x)
    flipped = [z, z + 1 - 2 * lax.rem(z, 2), lax.rem(z + 2, 4), 3 - z]
    over_z = [(r, 2 * f + x) for f in flipped]
    own_rows = pl.multiple_of(k * mine, 16)
    sib_rows = pl.multiple_of((1 - k) * mine, 16)

    loads = [
        pltpu.make_async_copy(src, dst, load_sem.at[i])
        for i, (src, dst) in enumerate(
            [(in_ref, got.at[0, 0]), (cot_ref, got.at[0, 1]), (wg_hbm, wg), (wu_hbm, wu), (wd_hbm, wd)]
        )
    ]
    for load in loads:
        load.start()

    barrier = pltpu.get_barrier_semaphore()
    partners = [sibling, over_y, over_x] + over_z[1:]
    for partner in partners:
        pl.semaphore_signal(barrier, inc=1, device_id=partner, device_id_type=MESH)
    pl.semaphore_wait(barrier, len(partners))

    def remote(src, dst, ss, rs, device):
        return pltpu.make_async_remote_copy(
            src_ref=src, dst_ref=dst, send_sem=ss, recv_sem=rs, device_id=device, device_id_type=MESH
        )

    middle = jnp.logical_and(z > 0, z < 3)
    own_near = remote(got.at[0], got.at[2], z_ss.at[0], z_rs.at[1], over_z[1])
    own_far = remote(got.at[0], got.at[6], z_ss.at[1], z_rs.at[3], over_z[3])
    near_far = remote(got.at[2], got.at[4], z_ss.at[2], z_rs.at[2], over_z[3])
    far_near = remote(got.at[6], got.at[4], z_ss.at[3], z_rs.at[2], over_z[1])
    last_near = remote(got.at[4], got.at[6], z_ss.at[4], z_rs.at[3], over_z[1])
    to_x = [
        remote(got.at[2 * d], got.at[2 * d + 1], x_ss.at[d], x_rs.at[d], over_x) for d in range(4)
    ]

    loads[0].wait()
    loads[1].wait()
    own_near.start()

    @pl.when(middle)
    def _():
        own_far.start()

    to_x[0].start()
    own_near.wait_recv()

    @pl.when(middle)
    def _():
        near_far.start()

    to_x[1].start()

    @pl.when(middle)
    def _():
        own_far.wait_recv()
        far_near.start()
        to_x[3].start()
        near_far.wait_recv()
        last_near.start()
        to_x[2].start()

    @pl.when(jnp.logical_not(middle))
    def _():
        near_far.wait_recv()
        to_x[2].start()

    def settle(h):
        at = pl.ds(h * half, half)
        for i, whole in enumerate((xs, cs)):
            whole[at, :] = jnp.concatenate(
                [got[4 * h + s, i].astype(F32) for s in range(4)], axis=0
            ).astype(BF16)

    def to_sibling(h, j):
        return remote(
            part.at[h, j, :, pl.ds(sib_rows, mine), :], sib_got.at[h, j],
            p_ss.at[h, j], p_rs.at[h, j], sibling,
        )

    def to_y(h, j):
        return remote(y_send.at[h, j], y_got.at[h, j], y_ss.at[h, j], y_rs.at[h, j], over_y)

    def act_to_sibling(h, j):
        at = act.at[:, pl.ds(pl.multiple_of(h * half + own_rows, 16), mine), pl.ds(pl.multiple_of(j * TILE, TILE), TILE)]
        return remote(at, at, a_ss.at[h, j], a_rs.at[h, j], sibling)

    def forward(h, first, last):
        at = pl.ds(h * half, half)

        @pl.loop(first, last)
        def _(j):
            cols = pl.ds(pl.multiple_of(j * TILE, TILE), TILE)
            part[h, j, 0] = jnp.dot(xs[at, :], wg[:, cols], preferred_element_type=F32)
            part[h, j, 1] = jnp.dot(xs[at, :], wu[:, cols], preferred_element_type=F32)
            part[h, j, 2] = contract_cols(cs[at, :], wd[cols, :])
            to_sibling(h, j).start()

    def reduce_cores(h):
        @pl.loop(0, tiles)
        def _(j):
            to_sibling(h, j).wait_recv()
            total = part[h, j, :, pl.ds(own_rows, mine), :] + sib_got[h, j]
            part[h, j, :, pl.ds(own_rows, mine), :] = total
            y_send[h, j] = total.astype(BF16)
            to_y(h, j).start()

    def grad_to_x(d):
        return remote(rx_send.at[d], rx_got.at[d], gx_ss.at[d], gx_rs.at[d], over_x)

    def grad_to_z(d):
        return remote(rz_send.at[d], rz_got.at[d], gz_ss.at[d], gz_rs.at[d], over_z[d])

    def activate(h, j):
        to_y(h, j).wait_recv()
        total = part[h, j, :, pl.ds(own_rows, mine), :] + y_got[h, j].astype(F32)
        rows = pl.ds(pl.multiple_of(h * half + own_rows, 16), mine)
        cols = pl.ds(pl.multiple_of(j * TILE, TILE), TILE)
        for m, value in enumerate(activations(total[0], total[1], total[2])):
            act[m, rows, cols] = value
        act_to_sibling(h, j).start()

    def accumulate(h, j):
        act_to_sibling(h, j).wait_recv()
        cols = pl.ds(pl.multiple_of(j * TILE, TILE), TILE)
        grad_gate = act[0, pl.ds(h * half, half), cols]
        grad_up = act[1, pl.ds(h * half, half), cols]
        for n in range(width // TILE):
            out = pl.ds(n * TILE, TILE)
            grads[:, out] += contract_cols(grad_gate, wg[out, cols]) + contract_cols(grad_up, wu[out, cols])

    def backward(h):
        grads[...] = jnp.zeros_like(grads)
        activate(h, 0)

        @pl.loop(1, tiles)
        def _(j):
            activate(h, j)
            accumulate(h, j - 1)

        accumulate(h, tiles - 1)
        for e in (1, 0):
            d = 2 * h + e
            rx_send[d] = grads[(2 * e + 1) * shard : (2 * e + 2) * shard, :].astype(BF16)
            grad_to_x(d).start()
            keep[d] = grads[2 * e * shard : (2 * e + 1) * shard, :]

    def reduce_x(h):
        for e in (1, 0):
            d = 2 * h + e
            grad_to_x(d).wait_recv()
            total = keep[d] + rx_got[d].astype(F32)
            if d == 0:
                keep[d] = total
            else:
                rz_send[d] = total.astype(BF16)
                grad_to_z(d).start()

    to_x[0].wait_recv()
    to_x[1].wait_recv()
    settle(0)
    for load in loads[2:]:
        load.wait()
    forward(0, 0, tiles // 2)

    @pl.when(jnp.logical_not(middle))
    def _():
        own_far.wait_recv()
        to_x[3].start()

    forward(0, tiles // 2, tiles)
    reduce_cores(0)
    to_x[3].wait_recv()
    to_x[2].wait_recv()
    settle(1)
    outs = [
        pltpu.make_async_copy(src, dst, out_sem.at[i])
        for i, (src, dst) in enumerate([(xs, x_out), (cs, c_out), (act, act_out)])
    ]
    outs[0].start()
    outs[1].start()
    forward(1, 0, tiles)
    reduce_cores(1)
    backward(0)
    reduce_x(0)
    backward(1)
    outs[2].start()
    reduce_x(1)
    total = keep[0]
    for d in (1, 3, 2):
        grad_to_z(d).wait_recv()
        total += rz_got[d].astype(F32)
    gi_ref[...] = total.astype(BF16)

    own_near.wait_send()

    @pl.when(middle)
    def _():
        for copy in (own_far, near_far, far_near, last_near):
            copy.wait_send()

    for d in (1, 2, 3):
        grad_to_z(d).wait_send()
    for d in range(4):
        to_x[d].wait_send()
        grad_to_x(d).wait_send()
    for h in range(2):
        @pl.loop(0, tiles)
        def _(j):
            to_sibling(h, j).wait_send()
            to_y(h, j).wait_send()
            act_to_sibling(h, j).wait_send()
    for out in outs:
        out.wait()


def weights_kernel(xs, cs, act, gate_hbm, up_hbm, down_hbm, gate_buf, up_buf, down_buf, sem):
    blocks, down_blocks = xs.shape[1] // TILE, act.shape[2] // TILE

    def writes(i):
        at = pl.ds(pl.multiple_of(i * TILE, TILE), TILE)
        slot = lax.rem(i, 2)
        return [
            pltpu.make_async_copy(buf.at[slot], hbm.at[at, :], sem.at[n, slot])
            for n, (buf, hbm) in enumerate([(gate_buf, gate_hbm), (up_buf, up_hbm), (down_buf, down_hbm)])
        ]

    def block(i, count):
        at = pl.ds(pl.multiple_of(i * TILE, TILE), TILE)
        slot = lax.rem(i, 2)
        copies = writes(i)[:count]

        @pl.when(i >= 2)
        def _():
            for copy in writes(i - 2)[:count]:
                copy.wait()

        rows = xs[:, at].T
        gate_buf[slot] = jnp.dot(rows, act[0], preferred_element_type=F32).astype(BF16)
        copies[0].start()
        up_buf[slot] = jnp.dot(rows, act[1], preferred_element_type=F32).astype(BF16)
        copies[1].start()
        if count == 3:
            down_buf[slot] = jnp.dot(act[2, :, at].T, cs[...], preferred_element_type=F32).astype(BF16)
            copies[2].start()

    @pl.loop(0, down_blocks)
    def _(i):
        block(i, 3)

    for i in range(down_blocks, blocks):
        block(jnp.int32(i), 2)
    for i in (blocks - 2, blocks - 1):
        for copy in writes(jnp.int32(i))[:2]:
            copy.wait()
    for i in (down_blocks - 2, down_blocks - 1):
        writes(jnp.int32(i))[2].wait()


def fused(inputs, w_gate, w_up, w_down, cotangent):
    shard, width = inputs.shape
    columns = w_gate.shape[1]
    tokens = 8 * shard
    half, mine, tiles = tokens // 2, tokens // 4, columns // TILE
    dma = pltpu.SemaphoreType.DMA
    hbm = pl.BlockSpec(memory_space=pl.ANY)
    xs, cs, act, grad_inputs = pl.pallas_call(
        block_kernel,
        out_shape=(
            jax.ShapeDtypeStruct((tokens, width), BF16),
            jax.ShapeDtypeStruct((tokens, width), BF16),
            jax.ShapeDtypeStruct((3, tokens, columns), BF16),
            jax.ShapeDtypeStruct((shard, width), BF16),
        ),
        in_specs=[hbm] * 5,
        out_specs=(hbm, hbm, hbm, pl.BlockSpec(memory_space=pltpu.VMEM)),
        scratch_shapes=[
            pltpu.VMEM((8, 2, shard, width), BF16),
            pltpu.VMEM(w_gate.shape, BF16),
            pltpu.VMEM(w_up.shape, BF16),
            pltpu.VMEM(w_down.shape, BF16),
            pltpu.VMEM((tokens, width), BF16),
            pltpu.VMEM((tokens, width), BF16),
            pltpu.VMEM((2, tiles, 3, half, TILE), F32),
            pltpu.VMEM((2, tiles, 3, mine, TILE), F32),
            pltpu.VMEM((2, tiles, 3, mine, TILE), BF16),
            pltpu.VMEM((2, tiles, 3, mine, TILE), BF16),
            pltpu.VMEM((3, tokens, columns), BF16),
            pltpu.VMEM((half, width), F32),
            pltpu.VMEM((4, shard, width), F32),
            pltpu.VMEM((4, shard, width), BF16),
            pltpu.VMEM((4, shard, width), BF16),
            pltpu.VMEM((4, shard, width), BF16),
            pltpu.VMEM((4, shard, width), BF16),
            dma((5,)), dma((3,)), dma((5,)), dma((4,)), dma((4,)), dma((4,)),
            dma((2, tiles)), dma((2, tiles)), dma((2, tiles)), dma((2, tiles)),
            dma((2, tiles)), dma((2, tiles)),
            dma((4,)), dma((4,)), dma((4,)), dma((4,)),
        ],
        compiler_params=pltpu.CompilerParams(
            collective_id=0, has_side_effects=True, vmem_limit_bytes=56 * 2**20
        ),
        name="swiglu_block",
    )(inputs, cotangent, w_gate, w_up, w_down)
    vmem = pl.BlockSpec(memory_space=pltpu.VMEM)
    grad_gate, grad_up, grad_down = pl.pallas_call(
        weights_kernel,
        out_shape=(
            jax.ShapeDtypeStruct((width, columns), BF16),
            jax.ShapeDtypeStruct((width, columns), BF16),
            jax.ShapeDtypeStruct((columns, width), BF16),
        ),
        in_specs=[vmem] * 3,
        out_specs=(hbm,) * 3,
        scratch_shapes=[
            pltpu.VMEM((2, TILE, columns), BF16),
            pltpu.VMEM((2, TILE, columns), BF16),
            pltpu.VMEM((2, TILE, width), BF16),
            dma((3, 2)),
        ],
        compiler_params=pltpu.CompilerParams(vmem_limit_bytes=40 * 2**20),
        name="weight_grads",
    )(xs, cs, act)
    return grad_inputs, grad_gate, grad_up, grad_down


def solution(mesh):
    placed = (P("col", "row"), P("row", "col"), P("row", "col"), P("col", "row"), P("col", "row"))
    small = mesh.shape["row"] == 4 and mesh.shape["col"] == 8
    return jax.shard_map(
        fused if small else on_device,
        mesh=mesh,
        in_specs=placed,
        out_specs=(P("col", "row"), P("row", "col"), P("row", "col"), P("col", "row")),
        check_vma=False,
    )
```

```python
import functools

import jax
import jax.numpy as jnp
from jax import lax
from jax.experimental import pallas as pl
from jax.experimental.pallas import tpu as pltpu
from jax.sharding import PartitionSpec as P

MESH = pl.DeviceIdType.MESH
BF16, F32 = jnp.bfloat16, jnp.float32
TILE = 256


def contract_rows(left, right):
    return lax.dot_general(
        left, right, (((0,), (0,)), ((), ())), preferred_element_type=jnp.float32
    )


def contract_cols(left, right):
    return lax.dot_general(
        left, right, (((1,), (1,)), ((), ())), preferred_element_type=jnp.float32
    )


def activations(gate_sum, up_sum, grad_hidden):
    sigmoid_gate = jax.nn.sigmoid(gate_sum)
    activated = gate_sum * sigmoid_gate
    hidden = (activated * up_sum).astype(BF16)
    grad_gate_act = (
        grad_hidden * up_sum * sigmoid_gate * (1.0 + gate_sum * (1.0 - sigmoid_gate))
    ).astype(BF16)
    grad_up_act = (grad_hidden * activated).astype(BF16)
    return grad_gate_act, grad_up_act, hidden


def on_device(inputs, w_gate, w_up, w_down, cotangent):
    rows_in = lax.all_gather(inputs, "col", axis=0, tiled=True)
    rows_co = lax.all_gather(cotangent, "col", axis=0, tiled=True)
    columns = w_gate.shape[1]
    gate_part = jnp.dot(rows_in, w_gate, preferred_element_type=jnp.float32)
    up_part = jnp.dot(rows_in, w_up, preferred_element_type=jnp.float32)
    back_part = contract_cols(rows_co, w_down)
    summed = lax.psum_scatter(
        jnp.concatenate([gate_part, up_part, back_part], axis=1),
        "row",
        scatter_dimension=0,
        tiled=True,
    )
    acts = activations(
        summed[:, :columns], summed[:, columns : 2 * columns], summed[:, 2 * columns :]
    )
    piece_gate, piece_up, piece_hidden = [
        lax.all_gather(act, "row", axis=0, tiled=True) for act in acts
    ]
    acc_gate = contract_rows(rows_in, piece_gate)
    acc_up = contract_rows(rows_in, piece_up)
    acc_down = contract_rows(piece_hidden, rows_co)
    acc_inputs = contract_cols(piece_gate, w_gate) + contract_cols(piece_up, w_up)
    grad_inputs = lax.psum_scatter(acc_inputs, "col", scatter_dimension=0, tiled=True)
    return (
        grad_inputs.astype(BF16),
        acc_gate.astype(BF16),
        acc_up.astype(BF16),
        acc_down.astype(BF16),
    )


def block_kernel(
    in_ref, cot_ref, wg_hbm, wu_hbm, wd_hbm,
    x_out, c_out, act_out, own_ref, two_ref, three_ref,
    got, wg, wu, wd, xs, cs, part, sib_got, y_send, y_got, act,
    grads, keep, rx_send, rx_got, rz_send, rz_got,
    load_sem, out_sem, z_ss, z_rs, x_ss, x_rs, p_ss, p_rs, y_ss, y_rs, a_ss, a_rs,
    gx_ss, gx_rs, gz_ss, gz_rs,
):
    shard, width = in_ref.shape
    half = 4 * shard
    mine = half // 2
    tiles = wg.shape[1] // TILE
    r, c = lax.axis_index("row"), lax.axis_index("col")
    k, x, z = lax.rem(r, 2), lax.rem(c, 2), lax.div(c, 2)
    sibling = (r + 1 - 2 * k, c)
    over_y = (lax.rem(r + 2, 4), c)
    over_x = (r, c + 1 - 2 * x)
    flipped = [z, z + 1 - 2 * lax.rem(z, 2), lax.rem(z + 2, 4), 3 - z]
    over_z = [(r, 2 * f + x) for f in flipped]
    own_rows = pl.multiple_of(k * mine, 16)
    sib_rows = pl.multiple_of((1 - k) * mine, 16)

    loads = [
        pltpu.make_async_copy(src, dst, load_sem.at[i])
        for i, (src, dst) in enumerate(
            [(in_ref, got.at[0, 0]), (cot_ref, got.at[0, 1]), (wg_hbm, wg), (wu_hbm, wu), (wd_hbm, wd)]
        )
    ]
    for load in loads:
        load.start()

    barrier = pltpu.get_barrier_semaphore()
    partners = [sibling, over_y, over_x, over_z[1], over_z[3]]
    for partner in partners:
        pl.semaphore_signal(barrier, inc=1, device_id=partner, device_id_type=MESH)
    pl.semaphore_wait(barrier, len(partners))

    def remote(src, dst, ss, rs, device):
        return pltpu.make_async_remote_copy(
            src_ref=src, dst_ref=dst, send_sem=ss, recv_sem=rs, device_id=device, device_id_type=MESH
        )

    middle = jnp.logical_and(z > 0, z < 3)
    own_near = remote(got.at[0], got.at[2], z_ss.at[0], z_rs.at[1], over_z[1])
    own_far = remote(got.at[0], got.at[6], z_ss.at[1], z_rs.at[3], over_z[3])
    near_far = remote(got.at[2], got.at[4], z_ss.at[2], z_rs.at[2], over_z[3])
    far_near = remote(got.at[6], got.at[4], z_ss.at[3], z_rs.at[2], over_z[1])
    last_near = remote(got.at[4], got.at[6], z_ss.at[4], z_rs.at[3], over_z[1])
    to_x = [
        remote(got.at[2 * d], got.at[2 * d + 1], x_ss.at[d], x_rs.at[d], over_x) for d in range(4)
    ]

    loads[0].wait()
    loads[1].wait()
    own_near.start()

    @pl.when(middle)
    def _():
        own_far.start()

    to_x[0].start()
    own_near.wait_recv()

    @pl.when(middle)
    def _():
        near_far.start()

    to_x[1].start()

    @pl.when(middle)
    def _():
        own_far.wait_recv()
        far_near.start()
        to_x[3].start()
        near_far.wait_recv()
        last_near.start()
        to_x[2].start()

    @pl.when(jnp.logical_not(middle))
    def _():
        near_far.wait_recv()
        to_x[2].start()

    def settle(h):
        at = pl.ds(h * half, half)
        for i, whole in enumerate((xs, cs)):
            whole[at, :] = jnp.concatenate(
                [got[4 * h + s, i].astype(F32) for s in range(4)], axis=0
            ).astype(BF16)

    def to_sibling(h, j):
        return remote(
            part.at[h, j, :, pl.ds(sib_rows, mine), :], sib_got.at[h, j],
            p_ss.at[h, j], p_rs.at[h, j], sibling,
        )

    def to_y(h, j):
        return remote(y_send.at[h, j], y_got.at[h, j], y_ss.at[h, j], y_rs.at[h, j], over_y)

    def act_to_sibling(h, j):
        at = act.at[:, pl.ds(pl.multiple_of(h * half + own_rows, 16), mine), pl.ds(pl.multiple_of(j * TILE, TILE), TILE)]
        return remote(at, at, a_ss.at[h, j], a_rs.at[h, j], sibling)

    def forward(h, first, last):
        at = pl.ds(h * half, half)

        @pl.loop(first, last)
        def _(j):
            cols = pl.ds(pl.multiple_of(j * TILE, TILE), TILE)
            part[h, j, 0] = jnp.dot(xs[at, :], wg[:, cols], preferred_element_type=F32)
            part[h, j, 1] = jnp.dot(xs[at, :], wu[:, cols], preferred_element_type=F32)
            part[h, j, 2] = contract_cols(cs[at, :], wd[cols, :])
            to_sibling(h, j).start()

    def reduce_cores(h):
        @pl.loop(0, tiles)
        def _(j):
            to_sibling(h, j).wait_recv()
            total = part[h, j, :, pl.ds(own_rows, mine), :] + sib_got[h, j]
            part[h, j, :, pl.ds(own_rows, mine), :] = total
            y_send[h, j] = total.astype(BF16)
            to_y(h, j).start()

    def grad_to_x(d):
        return remote(rx_send.at[d], rx_got.at[d], gx_ss.at[d], gx_rs.at[d], over_x)

    grad_to_z = remote(rz_send, rz_got, gz_ss, gz_rs, over_z[1])

    def activate(h, j):
        to_y(h, j).wait_recv()
        total = part[h, j, :, pl.ds(own_rows, mine), :] + y_got[h, j].astype(F32)
        rows = pl.ds(pl.multiple_of(h * half + own_rows, 16), mine)
        cols = pl.ds(pl.multiple_of(j * TILE, TILE), TILE)
        for m, value in enumerate(activations(total[0], total[1], total[2])):
            act[m, rows, cols] = value
        act_to_sibling(h, j).start()

    def accumulate(h, j):
        act_to_sibling(h, j).wait_recv()
        cols = pl.ds(pl.multiple_of(j * TILE, TILE), TILE)
        grad_gate = act[0, pl.ds(h * half, half), cols]
        grad_up = act[1, pl.ds(h * half, half), cols]
        for n in range(width // TILE):
            out = pl.ds(n * TILE, TILE)
            grads[:, out] += contract_cols(grad_gate, wg[out, cols]) + contract_cols(grad_up, wu[out, cols])

    def backward(h):
        grads[...] = jnp.zeros_like(grads)
        activate(h, 0)

        @pl.loop(1, tiles)
        def _(j):
            activate(h, j)
            accumulate(h, j - 1)

        accumulate(h, tiles - 1)
        for e in (1, 0):
            d = 2 * h + e
            rx_send[d] = grads[(2 * e + 1) * shard : (2 * e + 2) * shard, :].astype(BF16)
            grad_to_x(d).start()
            keep[d] = grads[2 * e * shard : (2 * e + 1) * shard, :]

    def reduce_x(h):
        for e in (1, 0):
            d = 2 * h + e
            grad_to_x(d).wait_recv()
            total = keep[d] + rx_got[d].astype(F32)
            if d == 0:
                keep[d] = total
            elif d == 1:
                rz_send[...] = total.astype(BF16)
                grad_to_z.start()
            else:
                (two_ref if d == 2 else three_ref)[...] = total.astype(BF16)

    to_x[0].wait_recv()
    to_x[1].wait_recv()
    settle(0)
    for load in loads[2:]:
        load.wait()
    forward(0, 0, tiles // 2)

    @pl.when(jnp.logical_not(middle))
    def _():
        own_far.wait_recv()
        to_x[3].start()

    forward(0, tiles // 2, tiles)
    reduce_cores(0)
    to_x[3].wait_recv()
    to_x[2].wait_recv()
    settle(1)
    outs = [
        pltpu.make_async_copy(src, dst, out_sem.at[i])
        for i, (src, dst) in enumerate([(xs, x_out), (cs, c_out), (act, act_out)])
    ]
    outs[0].start()
    outs[1].start()
    forward(1, 0, tiles)
    reduce_cores(1)
    backward(0)
    reduce_x(0)
    backward(1)
    outs[2].start()
    reduce_x(1)
    grad_to_z.wait_recv()
    own_ref[...] = keep[0] + rz_got[...].astype(F32)
    own_near.wait_send()

    @pl.when(middle)
    def _():
        for copy in (own_far, near_far, far_near, last_near):
            copy.wait_send()

    grad_to_z.wait_send()
    for d in range(4):
        to_x[d].wait_send()
        grad_to_x(d).wait_send()
    for h in range(2):
        @pl.loop(0, tiles)
        def _(j):
            to_sibling(h, j).wait_send()
            to_y(h, j).wait_send()
            act_to_sibling(h, j).wait_send()
    for out in outs:
        out.wait()


def weights_kernel(xs, cs, act, gate, up, down, *, down_blocks):
    i = pl.program_id(0)
    rows = xs[...].T
    gate[...] = jnp.dot(rows, act[0], preferred_element_type=F32).astype(BF16)
    up[...] = jnp.dot(rows, act[1], preferred_element_type=F32).astype(BF16)

    @pl.when(i < down_blocks)
    def _():
        at = pl.ds(pl.multiple_of(i * TILE, TILE), TILE)
        down[...] = jnp.dot(act[2, :, at].T, cs[...], preferred_element_type=F32).astype(BF16)


def fused(inputs, w_gate, w_up, w_down, cotangent):
    shard, width = inputs.shape
    columns = w_gate.shape[1]
    tokens = 8 * shard
    half, mine, tiles = tokens // 2, tokens // 4, columns // TILE
    dma = pltpu.SemaphoreType.DMA
    hbm, vmem = pl.BlockSpec(memory_space=pl.ANY), pl.BlockSpec(memory_space=pltpu.VMEM)
    xs, cs, act, own, two, three = pl.pallas_call(
        block_kernel,
        out_shape=(
            jax.ShapeDtypeStruct((tokens, width), BF16),
            jax.ShapeDtypeStruct((tokens, width), BF16),
            jax.ShapeDtypeStruct((3, tokens, columns), BF16),
            jax.ShapeDtypeStruct((shard, width), F32),
            jax.ShapeDtypeStruct((shard, width), BF16),
            jax.ShapeDtypeStruct((shard, width), BF16),
        ),
        in_specs=[hbm] * 5,
        out_specs=(hbm, hbm, hbm, vmem, vmem, vmem),
        scratch_shapes=[
            pltpu.VMEM((8, 2, shard, width), BF16),
            pltpu.VMEM(w_gate.shape, BF16),
            pltpu.VMEM(w_up.shape, BF16),
            pltpu.VMEM(w_down.shape, BF16),
            pltpu.VMEM((tokens, width), BF16),
            pltpu.VMEM((tokens, width), BF16),
            pltpu.VMEM((2, tiles, 3, half, TILE), F32),
            pltpu.VMEM((2, tiles, 3, mine, TILE), F32),
            pltpu.VMEM((2, tiles, 3, mine, TILE), BF16),
            pltpu.VMEM((2, tiles, 3, mine, TILE), BF16),
            pltpu.VMEM((3, tokens, columns), BF16),
            pltpu.VMEM((half, width), F32),
            pltpu.VMEM((4, shard, width), F32),
            pltpu.VMEM((4, shard, width), BF16),
            pltpu.VMEM((4, shard, width), BF16),
            pltpu.VMEM((shard, width), BF16),
            pltpu.VMEM((shard, width), BF16),
            dma((5,)), dma((3,)), dma((5,)), dma((4,)), dma((4,)), dma((4,)),
            dma((2, tiles)), dma((2, tiles)), dma((2, tiles)), dma((2, tiles)),
            dma((2, tiles)), dma((2, tiles)),
            dma((4,)), dma((4,)), dma(()), dma(()),
        ],
        compiler_params=pltpu.CompilerParams(
            collective_id=0, has_side_effects=True, vmem_limit_bytes=56 * 2**20
        ),
        name="swiglu_block",
    )(inputs, cotangent, w_gate, w_up, w_down)
    over_z = [
        [(2 * z + x, 2 * other + x) for z, other in enumerate(others) for x in range(2)]
        for others in ((2, 3, 0, 1), (3, 2, 1, 0))
    ]
    two = lax.ppermute(two, "col", over_z[0])
    three = lax.ppermute(three, "col", over_z[1])
    blocks, down_blocks = width // TILE, columns // TILE
    grad_gate, grad_up, grad_down = pl.pallas_call(
        functools.partial(weights_kernel, down_blocks=down_blocks),
        grid=(blocks,),
        out_shape=(
            jax.ShapeDtypeStruct((width, columns), BF16),
            jax.ShapeDtypeStruct((width, columns), BF16),
            jax.ShapeDtypeStruct((columns, width), BF16),
        ),
        in_specs=[
            pl.BlockSpec((tokens, TILE), lambda i: (0, i)),
            pl.BlockSpec((tokens, width), lambda i: (0, 0)),
            pl.BlockSpec((3, tokens, columns), lambda i: (0, 0, 0)),
        ],
        out_specs=(
            pl.BlockSpec((TILE, columns), lambda i: (i, 0)),
            pl.BlockSpec((TILE, columns), lambda i: (i, 0)),
            pl.BlockSpec((TILE, width), lambda i: (jnp.minimum(i, down_blocks - 1), 0)),
        ),
        compiler_params=pltpu.CompilerParams(vmem_limit_bytes=60 * 2**20),
        cost_estimate=pl.CostEstimate(
            flops=6 * tokens * width * columns,
            bytes_accessed=2 * (3 * width * columns + tokens * (2 * width + 3 * columns)),
            transcendentals=0,
        ),
        name="weight_grads",
    )(xs, cs, act)
    grad_inputs = (own + two.astype(F32) + three.astype(F32)).astype(BF16)
    return grad_inputs, grad_gate, grad_up, grad_down


def solution(mesh):
    placed = (P("col", "row"), P("row", "col"), P("row", "col"), P("col", "row"), P("col", "row"))
    small = mesh.shape["row"] == 4 and mesh.shape["col"] == 8
    return jax.shard_map(
        fused if small else on_device,
        mesh=mesh,
        in_specs=placed,
        out_specs=(P("col", "row"), P("row", "col"), P("row", "col"), P("col", "row")),
        check_vma=False,
    )
```
